32 devices in a mesh: groups: 2 (over y), node: 4 (over x, core), local: 4 (over z).
Axes of the slice: x: 2, y: 2, z: 4, core: 2. Of those that a mesh axis runs over, the one named last changes fastest.
Arguments:
- tokens_in: bfloat16 [2, 2048, 3584], P(None, ('groups', 'node', 'local')), parts along dimension 1, may hold values from -6 to 6
- expert_ids: int32 [2, 2048, 4], P(None, ('groups', 'node', 'local')), parts along dimension 1, may hold values from 0 to 7, as said below
- gate_fixed: int32 [2, 2048, 4], P(None, ('groups', 'node', 'local')), parts along dimension 1, may hold values from 1 to 65535
- w_gate: bfloat16 [16, 3584, 512], P(('node', 'local')), may hold values from -0.09375 to 0.09375
- w_up: bfloat16 [16, 3584, 512], P(('node', 'local')), may hold values from -0.09375 to 0.09375
- w_down: bfloat16 [16, 512, 3584], P(('node', 'local')), may hold values from -0.1875 to 0.1875
Outputs:
- mixed: bfloat16 [2, 2048, 3584], P(None, ('groups', 'node', 'local')), parts along dimension 1
The draws below stay inside these ranges and needn't reach their ends.
There are 2 independent parts, one for each index of `groups`. The reference program is written for one: setup_inputs(seed, part) draws one part's arguments, and reference() takes and returns one part's arrays. A program takes and returns all parts, laid end to end along the dimension named above; an argument that names none is the same for every part. Nothing has to cross between parts.
Inputs may be any that keep to these rules, and one draw needn't show every extreme that they name: `expert_ids`: each token names 4 different experts. Among the 64 tokens of one device in one micro-batch (aligned blocks of 64 tokens) no expert is named by more than 40 tokens, and one expert, the same in every block of a draw, is named by exactly 40.
All inputs are finite; a program needn't handle non-finite values.
Results may differ from the reference program's by a relative error of at most 0.0066.
Values may be sent and summed in bfloat16 or wider, within the bound.
A program may use at most 128 MiB of HBM per device.

```python
import jax
import jax.numpy as jnp
from jax import lax

D = 3584
FF = 1024
TOP = 4
MB = 2
TOK_DEV = 64
EXPERTS = 8
CAP = 40
TOKENS = 1024


def draw_expert_ids(key, part):
    key = jax.random.fold_in(key, 7)
    hot_key, bias_key, block_key = jax.random.split(key, 3)
    hot_expert = jax.random.randint(hot_key, (), 0, EXPERTS)
    expert_bias = jax.random.randint(bias_key, (EXPERTS,), 0, 4) * 256
    ticket_expert = jnp.repeat(jnp.arange(EXPERTS, dtype=jnp.int32), CAP)
    ticket_count = EXPERTS * CAP
    block_count = MB * TOKENS // TOK_DEV

    def one_block(single_key):
        score_key, token_key, order_key = jax.random.split(single_key, 3)
        score = jax.random.randint(score_key, (ticket_count,), 0, 1024) + expert_bias[ticket_expert]
        score = score + jnp.where(ticket_expert == hot_expert, 1 << 20, 0)
        score = score * ticket_count + jnp.arange(ticket_count, dtype=jnp.int32)
        kept_score, kept_index = lax.top_k(score, TOK_DEV * TOP)
        sorted_experts = jnp.sort(ticket_expert[kept_index])
        assigned = sorted_experts.reshape(TOP, TOK_DEV).T
        assigned = assigned[jax.random.permutation(token_key, TOK_DEV)]
        order_score = jax.random.randint(order_key, (TOK_DEV, TOP), 0, 1 << 20) * TOP + jnp.arange(TOP, dtype=jnp.int32)[None, :]
        order = jnp.argsort(order_score, axis=1)
        return jnp.take_along_axis(assigned, order, axis=1)
    tables = jax.vmap(one_block)(jax.random.split(block_key, block_count))
    return tables.reshape(MB, TOKENS, TOP).astype(jnp.int32)


def place_ends(array, key, smallest, largest):
    place = [jax.random.randint(jax.random.fold_in(key, axis), (), 0, length) for axis, length in enumerate(array.shape)]
    main_axis = array.shape.index(max(array.shape))
    next_to = place[:main_axis] + [(place[main_axis] + 1) % array.shape[main_axis]] + place[main_axis + 1:]
    return array.at[tuple(place)].set(smallest).at[tuple(next_to)].set(largest)


def level_of(key, extent, shards, least, high):
    loudness = 1.0
    for dim, parts in shards:
        draws = jax.random.uniform(jax.random.fold_in(jax.random.fold_in(key, 6), dim), (parts,), jnp.float32, least / len(shards), high / len(shards))
        loudness = loudness * jnp.repeat(jnp.exp(draws), extent[dim] // parts).reshape((-1,) + (1,) * (len(extent) - 1 - dim))
    return loudness


def noise(own_key, dims, width, reach, cuts=(), kind=jnp.bfloat16):
    array = jax.random.normal(own_key, dims, jnp.float32) * width
    if len(cuts) > 0:
        array = level_of(own_key, dims, cuts, -0.22, 0.18) * array
    return jnp.clip(array, min=-reach, max=reach).astype(kind)


def setup_inputs(seed: int = 0, part: int = 0) -> dict:
    keys = jax.random.split(jax.random.key(seed), 7)
    part_splits = jax.random.split(jax.random.fold_in(keys[6], part), 7)
    tokens_in = noise(part_splits[0], (MB, TOKENS, D), 1.0, 6.0, ((1, 16),))
    expert_ids = draw_expert_ids(jax.random.fold_in(jax.random.fold_in(keys[6], part), 71), part)
    gate_fixed = place_ends(jax.random.randint(part_splits[2], (MB, TOKENS, TOP), 1, 65536), jax.random.fold_in(part_splits[2], 1), 1, 65535).astype(jnp.int32)
    w_gate = noise(keys[3], (2 * EXPERTS, D, FF // 2), D ** -0.5, 0.09375, ((0, 16),))
    w_up = noise(keys[4], (2 * EXPERTS, D, FF // 2), D ** -0.5, 0.09375, ((0, 16),))
    w_down = noise(keys[5], (2 * EXPERTS, FF // 2, D), FF ** -0.5, 0.1875, ((0, 16),))
    return {"tokens_in": tokens_in, "expert_ids": expert_ids, "gate_fixed": gate_fixed, "w_gate": w_gate, "w_up": w_up, "w_down": w_down}


route_scale = 2.5


def reference(tokens_in, expert_ids, gate_fixed, w_gate, w_up, w_down):
    flat_rows = tokens_in.reshape(-1, D)
    chosen = expert_ids.reshape(-1, TOP)
    fixed_gate = gate_fixed.reshape(-1, TOP).astype(jnp.float32)
    weight = route_scale * fixed_gate / jnp.sum(fixed_gate, axis=1, keepdims=True)
    count_rows = flat_rows.shape[0]
    most_rows = (count_rows // TOK_DEV) * CAP

    def per_expert(running_total, expert):
        named = chosen == expert
        token_weight = jnp.sum(jnp.where(named, weight, 0.0), axis=1)
        used_rows = jnp.any(named, axis=1)
        picked = jnp.nonzero(used_rows, size=most_rows, fill_value=0)[0]
        live_rows = jnp.arange(most_rows) < jnp.sum(used_rows.astype(jnp.int32))
        expert_rows = flat_rows[picked]
        halves = []
        for half_index in range(2):
            weight_row = 2 * expert + half_index
            gate_act = jnp.dot(expert_rows, w_gate[weight_row], preferred_element_type=jnp.float32)
            up_act = jnp.dot(expert_rows, w_up[weight_row], preferred_element_type=jnp.float32)
            hidden = (jax.nn.silu(gate_act) * up_act).astype(jnp.bfloat16)
            halves.append(jnp.dot(hidden, w_down[weight_row], preferred_element_type=jnp.float32).astype(jnp.bfloat16))
        expert_out = (halves[0].astype(jnp.float32) + halves[1].astype(jnp.float32)).astype(jnp.bfloat16)
        row_scale = jnp.where(live_rows, token_weight[picked], jnp.float32(0.0))
        running_total = running_total.at[picked].add(row_scale[:, None] * expert_out.astype(jnp.float32))
        return running_total, None

    start_total = jnp.zeros((count_rows, D), jnp.float32)
    final_total, unused = lax.scan(per_expert, start_total, jnp.arange(EXPERTS))
    return final_total.astype(jnp.bfloat16).reshape(MB, TOKENS, D)
```

```python
import functools

import jax
import jax.numpy as jnp
from jax import lax
from jax.experimental import pallas as pl
from jax.experimental.pallas import tpu as pltpu
from jax.sharding import PartitionSpec as P

MESH = pl.DeviceIdType.MESH
lines_z = 4
rows_chunk = 256
cols_tile = 256

route_scale = 2.5


def expert_part(block, gate_half, up_half, down_half):
    block_shape = block.shape
    expert_rows = block.reshape(-1, block_shape[-1])
    gate_act = jnp.dot(expert_rows, gate_half, preferred_element_type=jnp.float32)
    up_act = jnp.dot(expert_rows, up_half, preferred_element_type=jnp.float32)
    hidden = (jax.nn.silu(gate_act) * up_act).astype(jnp.bfloat16)
    partial_out = jnp.dot(hidden, down_half, preferred_element_type=jnp.float32).astype(
        jnp.bfloat16
    )
    return partial_out.reshape(block_shape)


def shards(tokens_in, expert_ids, gate_fixed, w_gate, w_up, w_down):
    node_count = lax.axis_size("node")
    local_count = lax.axis_size("local")
    experts_node = local_count // 2
    experts = node_count * experts_node
    batches, tok_rows, width = tokens_in.shape
    top_count = expert_ids.shape[2]
    capacity = 5 * tok_rows * top_count // (4 * experts)
    gate_half = w_gate[0]
    up_half = w_up[0]
    down_half = w_down[0]
    results = []
    for micro_batch in range(batches):
        chosen = expert_ids[micro_batch]
        fixed_gate = gate_fixed[micro_batch].astype(jnp.float32)
        weight = route_scale * fixed_gate / jnp.sum(fixed_gate, axis=1, keepdims=True)
        onehot = (chosen[:, :, None] == jnp.arange(experts, dtype=jnp.int32)[None, None, :]).astype(
            jnp.int32
        )
        onehot = onehot.reshape(tok_rows * top_count, experts)
        before = jnp.cumsum(onehot, axis=0) - onehot
        slot_rank = jnp.sum(before * onehot, axis=1).reshape(tok_rows, top_count)
        position = chosen * capacity + slot_rank
        select = jnp.any(
            position[None, :, :] == jnp.arange(experts * capacity, dtype=jnp.int32)[:, None, None],
            axis=2,
        )
        packed = jnp.dot(
            select.astype(jnp.bfloat16), tokens_in[micro_batch], preferred_element_type=jnp.float32
        ).astype(jnp.bfloat16)
        blocks_grid = packed.reshape(node_count, experts_node, capacity, width)
        copies = jnp.repeat(blocks_grid, 2, axis=1).reshape(
            node_count * local_count, capacity, width
        )
        partial_value = expert_part(
            lax.all_to_all(copies, ("node", "local"), split_axis=0, concat_axis=0, tiled=True),
            gate_half,
            up_half,
            down_half,
        )
        partial_value = partial_value.reshape(node_count, local_count, capacity, width)
        returned = lax.all_to_all(
            partial_value.reshape(node_count * local_count, capacity, width),
            ("node", "local"),
            split_axis=0,
            concat_axis=0,
            tiled=True,
        )
        halves = returned.reshape(node_count, experts_node, 2, capacity, width).astype(jnp.float32)
        outputs = (halves[:, :, 0] + halves[:, :, 1]).astype(jnp.bfloat16)
        lookup = outputs.reshape(experts * capacity, width)
        picked = (
            lookup[position.reshape(-1)].reshape(tok_rows, top_count, width).astype(jnp.float32)
        )
        mixed = jnp.sum(weight[:, :, None] * picked, axis=1)
        results.append(mixed.astype(jnp.bfloat16))
    return jnp.stack(results)


z_steps = ((3, 1), (0, -1), (2, 1), (1, -1), (1, 1), (2, -1))


def gather_kernel(
    tokens, cols, gate_hbm, up_hbm, down_hbm, out,
    g, p, core_in, x_in, z_in, gate_w, up_w, down_w, hidden,
    load_sem, g_send, g_recv, c_send, c_recv, x_send, x_recv, z_send, z_recv,
):
    batches, tok, width = tokens.shape
    half_units = gate_w.shape[1]
    group = lax.axis_index("groups")
    node = lax.axis_index("node")
    z = lax.axis_index("local")
    x, core = node // 2, node % 2
    expert = node * (lines_z // 2) + z // 2
    other_x, other_core = 1 - x, 1 - core
    to_x = (group, other_x * 2 + core, z)
    to_core = (group, x * 2 + other_core, z)
    to_high = (group, node, z + 1)
    to_low = (group, node, z - 1)

    def slot(xs, zs, cs):
        return (xs * lines_z + zs) * 2 + cs

    def at_rows(index):
        return pl.ds(pl.multiple_of(index * tok, tok), tok)

    mine = slot(x, z, core)
    loads = []
    for batch in range(batches):
        loads.append(
            pltpu.make_async_copy(
                tokens.at[batch], g.at[batch, at_rows(mine), pl.ds(0, width)], load_sem.at[batch]
            )
        )
    loads.append(pltpu.make_async_copy(gate_hbm.at[0], gate_w, load_sem.at[2]))
    loads.append(pltpu.make_async_copy(up_hbm.at[0], up_w, load_sem.at[3]))
    loads.append(pltpu.make_async_copy(down_hbm.at[0], down_w, load_sem.at[4]))
    for load in loads:
        load.start()
    for batch in range(batches):
        g[batch, at_rows(mine), pl.ds(width, 128)] = cols[batch]

    barrier = pltpu.get_barrier_semaphore()
    pl.semaphore_signal(barrier, inc=1, device_id=to_x, device_id_type=MESH)
    pl.semaphore_signal(barrier, inc=1, device_id=to_core, device_id_type=MESH)

    @pl.when(z < lines_z - 1)
    def _():
        pl.semaphore_signal(barrier, inc=1, device_id=to_high, device_id_type=MESH)

    @pl.when(z > 0)
    def _():
        pl.semaphore_signal(barrier, inc=1, device_id=to_low, device_id_type=MESH)

    pl.semaphore_wait(barrier, 3 + (z + 1) % lines_z // 2)

    def g_copy(batch, index, kind, target):
        part = g.at[batch, at_rows(index)]
        return pltpu.make_async_remote_copy(
            src_ref=part, dst_ref=part,
            send_sem=g_send.at[batch, kind, index], recv_sem=g_recv.at[batch, index],
            device_id=target, device_id_type=MESH,
        )

    def arrived(batch, index):
        g_copy(batch, index, 3, to_core).wait_recv()

    def gather_own(batch):
        loads[batch].wait()
        g_copy(batch, mine, 2, to_x).start()

        @pl.when(z < lines_z - 1)
        def _():
            g_copy(batch, mine, 0, to_high).start()

        @pl.when(z > 0)
        def _():
            g_copy(batch, mine, 1, to_low).start()

        g_copy(batch, mine, 3, to_core).start()

    def gather_forward(batch, step):
        @pl.when(z >= step)
        def _():
            index = slot(x, z - step, core)
            arrived(batch, index)

            @pl.when(z < lines_z - 1)
            def _():
                g_copy(batch, index, 0, to_high).start()

            g_copy(batch, index, 2, to_x).start()
            g_copy(batch, index, 3, to_core).start()

        @pl.when(z + step < lines_z)
        def _():
            index = slot(x, z + step, core)
            arrived(batch, index)

            @pl.when(z > 0)
            def _():
                g_copy(batch, index, 1, to_low).start()

            g_copy(batch, index, 2, to_x).start()
            g_copy(batch, index, 3, to_core).start()

    def gather_across(batch):
        def one(zs):
            index = slot(other_x, zs, core)
            arrived(batch, index)
            g_copy(batch, index, 3, to_core).start()

        one(z)
        for step in range(1, lines_z):
            @pl.when(z >= step)
            def _():
                one(z - step)

            @pl.when(z + step < lines_z)
            def _():
                one(z + step)

    def gather_core(batch):
        @pl.loop(0, 2 * lines_z)
        def _(index):
            arrived(batch, index * 2 + other_core)

    def gather_sent(batch):
        @pl.loop(0, lines_z)
        def _(zs):
            index = slot(x, zs, core)

            @pl.when(jnp.logical_and(z < lines_z - 1, zs <= z))
            def _():
                g_copy(batch, index, 0, to_high).wait_send()

            @pl.when(jnp.logical_and(z > 0, zs >= z))
            def _():
                g_copy(batch, index, 1, to_low).wait_send()

            g_copy(batch, index, 2, to_x).wait_send()
            g_copy(batch, index, 3, to_core).wait_send()
            g_copy(batch, slot(other_x, zs, core), 3, to_core).wait_send()

    def compute(batch, xs, pair):
        first = pl.multiple_of((xs * lines_z + 2 * pair) * 2 * tok, rows_chunk)
        rows = pl.ds(first, rows_chunk)

        @pl.loop(0, half_units // cols_tile)
        def _(tile):
            at = pl.ds(pl.multiple_of(tile * cols_tile, cols_tile), cols_tile)
            block = g[batch, rows, pl.ds(0, width)]
            gate_act = jnp.dot(block, gate_w[:, at], preferred_element_type=jnp.float32)
            up_act = jnp.dot(block, up_w[:, at], preferred_element_type=jnp.float32)
            hidden[:, at] = (jax.nn.silu(gate_act) * up_act).astype(jnp.bfloat16)

        lane = lax.broadcasted_iota(jnp.int32, (rows_chunk, 128), 1)
        weights = g[batch, rows, pl.ds(width, 128)].astype(jnp.float32)
        chosen = jnp.logical_or(lane == expert, lane == expert + 64)
        scale = jnp.sum(jnp.where(chosen, weights, 0.0), axis=1, keepdims=True)

        @pl.loop(0, width // cols_tile)
        def _(tile):
            at = pl.ds(pl.multiple_of(tile * cols_tile, cols_tile), cols_tile)
            partial = jnp.dot(hidden[...], down_w[:, at], preferred_element_type=jnp.float32)
            p[batch, rows, at] = (partial * scale).astype(jnp.bfloat16)

        for zs in (2 * pair, 2 * pair + 1):
            core_copy(batch, xs, zs).start()

    def core_copy(batch, xs, zs):
        index = xs * lines_z + zs
        return pltpu.make_async_remote_copy(
            src_ref=p.at[batch, at_rows(slot(xs, zs, other_core))],
            dst_ref=core_in.at[batch, at_rows(index)],
            send_sem=c_send.at[batch, index], recv_sem=c_recv.at[batch, index],
            device_id=to_core, device_id_type=MESH,
        )

    def x_copy(batch, zs):
        return pltpu.make_async_remote_copy(
            src_ref=p.at[batch, at_rows(slot(other_x, zs, core))],
            dst_ref=x_in.at[batch, at_rows(zs)],
            send_sem=x_send.at[batch, zs], recv_sem=x_recv.at[batch, zs],
            device_id=to_x, device_id_type=MESH,
        )

    def z_copy(batch, zs, place, target):
        return pltpu.make_async_remote_copy(
            src_ref=p.at[batch, at_rows(slot(x, zs, core))],
            dst_ref=z_in.at[batch, at_rows(place)],
            send_sem=z_send.at[batch, zs], recv_sem=z_recv.at[batch, place],
            device_id=target, device_id_type=MESH,
        )

    def add(batch, index, source, place):
        @pl.loop(0, tok // 16)
        def _(part):
            to = pl.ds(pl.multiple_of(index * tok + part * 16, 16), 16)
            of = pl.ds(pl.multiple_of(place * tok + part * 16, 16), 16)
            total = p[batch, to, :].astype(jnp.float32) + source[batch, of, :].astype(jnp.float32)
            p[batch, to, :] = total.astype(jnp.bfloat16)

    def core_add(batch, xs, zs):
        core_copy(batch, xs, zs).wait_recv()
        add(batch, slot(xs, zs, core), core_in, xs * lines_z + zs)

    def in_order(body):
        for zs, way in z_steps:
            @pl.when(z < zs if way > 0 else z > zs)
            def _():
                body(zs, way)

    def send_x(batch):
        def one(zs, way):
            core_add(batch, other_x, zs)
            x_copy(batch, zs).start()

        in_order(one)
        one(z, 0)

    def keep_x(batch):
        @pl.loop(0, lines_z)
        def _(zs):
            core_add(batch, x, zs)

    def sum_z(batch):
        def one(zs, way):
            x_copy(batch, zs).wait_recv()
            index = slot(x, zs, core)
            add(batch, index, x_in, zs)
            if way > 0:
                @pl.when(z > 0)
                def _():
                    z_copy(batch, zs, zs, to_high).wait_recv()
                    add(batch, index, z_in, zs)

                z_copy(batch, zs, zs, to_high).start()
            else:
                @pl.when(z < lines_z - 1)
                def _():
                    z_copy(batch, zs, zs, to_low).wait_recv()
                    add(batch, index, z_in, zs)

                place = jnp.where(z == zs + 1, lines_z, zs)
                z_copy(batch, zs, place, to_low).start()

        in_order(one)
        x_copy(batch, z).wait_recv()
        add(batch, mine, x_in, z)

        @pl.when(z > 0)
        def _():
            z_copy(batch, z, z, to_high).wait_recv()
            add(batch, mine, z_in, z)

        @pl.when(z < lines_z - 1)
        def _():
            z_copy(batch, z, lines_z, to_low).wait_recv()
            add(batch, mine, z_in, lines_z)

        out[batch] = p[batch, at_rows(mine), :]

    def reduce_sent(batch):
        @pl.loop(0, lines_z)
        def _(zs):
            core_copy(batch, 0, zs).wait_send()
            core_copy(batch, 1, zs).wait_send()
            x_copy(batch, zs).wait_send()

            @pl.when(zs != z)
            def _():
                z_copy(batch, zs, zs, to_x).wait_send()

    gather_own(0)
    for step in range(1, lines_z):
        gather_forward(0, step)
    gather_own(1)
    gather_across(0)
    gather_core(0)
    for load in loads[2:]:
        load.wait()
    compute(0, other_x, 0)
    gather_forward(1, 1)
    compute(0, other_x, 1)
    gather_forward(1, 2)
    gather_forward(1, 3)
    send_x(0)
    compute(0, x, 0)
    compute(0, x, 1)
    keep_x(0)
    gather_across(1)
    gather_core(1)
    compute(1, other_x, 0)
    compute(1, other_x, 1)
    send_x(1)
    compute(1, x, 0)
    compute(1, x, 1)
    keep_x(1)
    sum_z(0)
    sum_z(1)
    for batch in range(batches):
        gather_sent(batch)
        reduce_sent(batch)


def gather_shards(tokens_in, expert_ids, gate_fixed, w_gate, w_up, w_down):
    batches, tok, width = tokens_in.shape
    half_units = w_gate.shape[2]
    fixed_gate = gate_fixed.astype(jnp.float32)
    weight = route_scale * fixed_gate / jnp.sum(fixed_gate, axis=2, keepdims=True)
    named = expert_ids[:, :, :, None] == jnp.arange(64, dtype=jnp.int32)
    dense = jnp.sum(jnp.where(named, weight[:, :, :, None], 0.0), axis=2)
    high = dense.astype(jnp.bfloat16)
    low = (dense - high.astype(jnp.float32)).astype(jnp.bfloat16)
    cols = jnp.concatenate([high, low], axis=2)
    total = 16 * tok
    bf16 = jnp.bfloat16
    dma = pltpu.SemaphoreType.DMA
    anywhere = pl.BlockSpec(memory_space=pl.ANY)
    vmem = pl.BlockSpec(memory_space=pltpu.VMEM)
    return pl.pallas_call(
        gather_kernel,
        out_shape=jax.ShapeDtypeStruct((batches, tok, width), bf16),
        in_specs=[anywhere, vmem, anywhere, anywhere, anywhere],
        out_specs=vmem,
        scratch_shapes=[
            pltpu.VMEM((batches, total, width + 128), bf16),
            pltpu.VMEM((batches, total, width), bf16),
            pltpu.VMEM((batches, 8 * tok, width), bf16),
            pltpu.VMEM((batches, 4 * tok, width), bf16),
            pltpu.VMEM((batches, 5 * tok, width), bf16),
            pltpu.VMEM((width, half_units), bf16),
            pltpu.VMEM((width, half_units), bf16),
            pltpu.VMEM((half_units, width), bf16),
            pltpu.VMEM((rows_chunk, half_units), bf16),
            dma((5,)),
            dma((batches, 4, 16)),
            dma((batches, 16)),
            dma((batches, 8)),
            dma((batches, 8)),
            dma((batches, 4)),
            dma((batches, 4)),
            dma((batches, 4)),
            dma((batches, 5)),
        ],
        compiler_params=pltpu.CompilerParams(
            collective_id=0, has_side_effects=True, vmem_limit_bytes=63 * 1024 * 1024
        ),
        cost_estimate=pl.CostEstimate(
            flops=6 * batches * total * width * half_units,
            bytes_accessed=3 * 2 * width * half_units,
            transcendentals=batches * total * half_units,
        ),
    )(tokens_in, cols, w_gate, w_up, w_down)


def solution(mesh):
    small = mesh.shape["node"] == 4 and mesh.shape["local"] == lines_z
    return jax.shard_map(
        gather_shards if small else shards,
        mesh=mesh,
        in_specs=(
            P(None, ("groups", "node", "local"), None),
            P(None, ("groups", "node", "local"), None),
            P(None, ("groups", "node", "local"), None),
            P(("node", "local"), None, None),
            P(("node", "local"), None, None),
            P(("node", "local"), None, None),
        ),
        out_specs=P(None, ("groups", "node", "local"), None),
        check_vma=False,
    )
```

```python
import functools

import jax
import jax.numpy as jnp
from jax import lax
from jax.experimental import pallas as pl
from jax.experimental.pallas import tpu as pltpu
from jax.sharding import PartitionSpec as P

MESH = pl.DeviceIdType.MESH
lines_z = 4
rows_chunk = 512
cols_tile = 512
side_cols = 256
side_gather = 384

route_scale = 2.5


def expert_part(block, gate_half, up_half, down_half):
    block_shape = block.shape
    expert_rows = block.reshape(-1, block_shape[-1])
    gate_act = jnp.dot(expert_rows, gate_half, preferred_element_type=jnp.float32)
    up_act = jnp.dot(expert_rows, up_half, preferred_element_type=jnp.float32)
    hidden = (jax.nn.silu(gate_act) * up_act).astype(jnp.bfloat16)
    partial_out = jnp.dot(hidden, down_half, preferred_element_type=jnp.float32).astype(
        jnp.bfloat16
    )
    return partial_out.reshape(block_shape)


def shards(tokens_in, expert_ids, gate_fixed, w_gate, w_up, w_down):
    node_count = lax.axis_size("node")
    local_count = lax.axis_size("local")
    experts_node = local_count // 2
    experts = node_count * experts_node
    batches, tok_rows, width = tokens_in.shape
    top_count = expert_ids.shape[2]
    capacity = 5 * tok_rows * top_count // (4 * experts)
    gate_half = w_gate[0]
    up_half = w_up[0]
    down_half = w_down[0]
    results = []
    for micro_batch in range(batches):
        chosen = expert_ids[micro_batch]
        fixed_gate = gate_fixed[micro_batch].astype(jnp.float32)
        weight = route_scale * fixed_gate / jnp.sum(fixed_gate, axis=1, keepdims=True)
        onehot = (chosen[:, :, None] == jnp.arange(experts, dtype=jnp.int32)[None, None, :]).astype(
            jnp.int32
        )
        onehot = onehot.reshape(tok_rows * top_count, experts)
        before = jnp.cumsum(onehot, axis=0) - onehot
        slot_rank = jnp.sum(before * onehot, axis=1).reshape(tok_rows, top_count)
        position = chosen * capacity + slot_rank
        select = jnp.any(
            position[None, :, :] == jnp.arange(experts * capacity, dtype=jnp.int32)[:, None, None],
            axis=2,
        )
        packed = jnp.dot(
            select.astype(jnp.bfloat16), tokens_in[micro_batch], preferred_element_type=jnp.float32
        ).astype(jnp.bfloat16)
        blocks_grid = packed.reshape(node_count, experts_node, capacity, width)
        copies = jnp.repeat(blocks_grid, 2, axis=1).reshape(
            node_count * local_count, capacity, width
        )
        partial_value = expert_part(
            lax.all_to_all(copies, ("node", "local"), split_axis=0, concat_axis=0, tiled=True),
            gate_half,
            up_half,
            down_half,
        )
        partial_value = partial_value.reshape(node_count, local_count, capacity, width)
        returned = lax.all_to_all(
            partial_value.reshape(node_count * local_count, capacity, width),
            ("node", "local"),
            split_axis=0,
            concat_axis=0,
            tiled=True,
        )
        halves = returned.reshape(node_count, experts_node, 2, capacity, width).astype(jnp.float32)
        outputs = (halves[:, :, 0] + halves[:, :, 1]).astype(jnp.bfloat16)
        lookup = outputs.reshape(experts * capacity, width)
        picked = (
            lookup[position.reshape(-1)].reshape(tok_rows, top_count, width).astype(jnp.float32)
        )
        mixed = jnp.sum(weight[:, :, None] * picked, axis=1)
        results.append(mixed.astype(jnp.bfloat16))
    return jnp.stack(results)


z_steps = ((3, 1), (0, -1), (2, 1), (1, -1), (1, 1), (2, -1))


def gather_kernel(
    tokens, cols, gate_hbm, up_hbm, down_hbm, out,
    g, p, core_in, x_in, z_in, b_in, gate_w, up_w, down_w, hidden,
    load_sem, g_send, g_recv, gb_recv, c_send, c_recv, x_send, x_recv, z_send, z_recv, b_send, b_recv,
):
    batches, tok, width = tokens.shape
    half_units = gate_w.shape[1]
    group = lax.axis_index("groups")
    node = lax.axis_index("node")
    z = lax.axis_index("local")
    x, core = node // 2, node % 2
    expert = node * (lines_z // 2) + z // 2
    other_x, other_core = 1 - x, 1 - core
    g_main = pl.ds(0, width + 128 - side_gather)
    g_side = pl.ds(width + 128 - side_gather, side_gather)
    p_main, p_side = pl.ds(0, width - side_cols), pl.ds(width - side_cols, side_cols)
    everything = pl.ds(0, width)
    to_x = (group, other_x * 2 + core, z)
    to_core = (group, x * 2 + other_core, z)
    to_high = (group, node, z + 1)
    to_low = (group, node, z - 1)

    def slot(xs, zs, cs):
        return (xs * lines_z + zs) * 2 + cs

    def at_rows(index):
        return pl.ds(pl.multiple_of(index * tok, tok), tok)

    mine = slot(x, z, core)
    loads = []
    for batch in range(batches):
        loads.append(
            pltpu.make_async_copy(
                tokens.at[batch], g.at[batch, at_rows(mine), pl.ds(0, width)], load_sem.at[batch]
            )
        )
    loads.append(pltpu.make_async_copy(gate_hbm.at[0], gate_w, load_sem.at[2]))
    loads.append(pltpu.make_async_copy(up_hbm.at[0], up_w, load_sem.at[3]))
    loads.append(pltpu.make_async_copy(down_hbm.at[0], down_w, load_sem.at[4]))
    for load in loads:
        load.start()
    for batch in range(batches):
        g[batch, at_rows(mine), pl.ds(width, 128)] = cols[batch]

    barrier = pltpu.get_barrier_semaphore()
    pl.semaphore_signal(barrier, inc=1, device_id=to_x, device_id_type=MESH)
    pl.semaphore_signal(barrier, inc=1, device_id=to_core, device_id_type=MESH)

    @pl.when(z < lines_z - 1)
    def _():
        pl.semaphore_signal(barrier, inc=1, device_id=to_high, device_id_type=MESH)

    @pl.when(z > 0)
    def _():
        pl.semaphore_signal(barrier, inc=1, device_id=to_low, device_id_type=MESH)

    pl.semaphore_wait(barrier, 3 + (z + 1) % lines_z // 2)

    def remote(part, to, send, recv, target):
        return pltpu.make_async_remote_copy(
            src_ref=part, dst_ref=to, send_sem=send, recv_sem=recv,
            device_id=target, device_id_type=MESH,
        )

    def g_copy(batch, index, kind, target):
        part = g.at[batch, at_rows(index)]
        return remote(part, part, g_send.at[batch, kind, index], g_recv.at[batch, index], target)

    def g_copy_main(batch, index):
        part = g.at[batch, at_rows(index), g_main]
        return remote(part, part, g_send.at[batch, 2, index], g_recv.at[batch, index], to_x)

    def g_copy_side(batch, index, kind, target):
        part = g.at[batch, at_rows(index), g_side]
        return remote(part, part, g_send.at[batch, kind, index], gb_recv.at[batch, index], target)

    def arrived(batch, index):
        g_copy(batch, index, 3, to_core).wait_recv()

    def both_ways(copy, batch, index):
        @pl.when(z < lines_z - 1)
        def _():
            copy(batch, index, 0, to_high).start()

        @pl.when(z > 0)
        def _():
            copy(batch, index, 1, to_low).start()

    def gather_own_x(batch):
        loads[batch].wait()
        g_copy(batch, mine, 2, to_x).start()

    def gather_own(batch):
        both_ways(g_copy, batch, mine)
        g_copy(batch, mine, 3, to_core).start()

    def gather_forward(batch, step):
        @pl.when(z >= step)
        def _():
            index = slot(x, z - step, core)
            arrived(batch, index)

            @pl.when(z < lines_z - 1)
            def _():
                g_copy(batch, index, 0, to_high).start()

            g_copy_main(batch, index).start()
            g_copy(batch, index, 3, to_core).start()

        @pl.when(z + step < lines_z)
        def _():
            index = slot(x, z + step, core)
            arrived(batch, index)

            @pl.when(z > 0)
            def _():
                g_copy(batch, index, 1, to_low).start()

            g_copy_main(batch, index).start()
            g_copy(batch, index, 3, to_core).start()

    def forward_side(batch, step):
        @pl.when(z >= step)
        def _():
            index = slot(other_x, z - step, core)
            g_copy_side(batch, index, 0, to_x).wait_recv()

            @pl.when(z < lines_z - 1)
            def _():
                g_copy_side(batch, index, 0, to_high).start()

        @pl.when(z + step < lines_z)
        def _():
            index = slot(other_x, z + step, core)
            g_copy_side(batch, index, 0, to_x).wait_recv()

            @pl.when(z > 0)
            def _():
                g_copy_side(batch, index, 1, to_low).start()

    def across_own(batch):
        index = slot(other_x, z, core)
        arrived(batch, index)
        both_ways(g_copy_side, batch, index)
        g_copy(batch, index, 3, to_core).start()

    def gather_across(batch, step):
        def one(zs):
            index = slot(other_x, zs, core)
            g_copy_main(batch, index).wait_recv()
            g_copy(batch, index, 3, to_core).start()

        @pl.when(z >= step)
        def _():
            one(z - step)

        @pl.when(z + step < lines_z)
        def _():
            one(z + step)

    def gather_core(batch, xs):
        @pl.loop(0, lines_z)
        def _(zs):
            arrived(batch, slot(xs, zs, other_core))

    def gather_sent(batch):
        @pl.loop(0, lines_z)
        def _(zs):
            index = slot(x, zs, core)
            across = slot(other_x, zs, core)

            @pl.when(jnp.logical_and(z < lines_z - 1, zs <= z))
            def _():
                g_copy(batch, index, 0, to_high).wait_send()
                g_copy_side(batch, across, 0, to_high).wait_send()

            @pl.when(jnp.logical_and(z > 0, zs >= z))
            def _():
                g_copy(batch, index, 1, to_low).wait_send()
                g_copy_side(batch, across, 1, to_low).wait_send()

            @pl.when(zs == z)
            def _():
                g_copy(batch, index, 2, to_x).wait_send()

            @pl.when(zs != z)
            def _():
                g_copy_main(batch, index).wait_send()

            g_copy(batch, index, 3, to_core).wait_send()
            g_copy(batch, across, 3, to_core).wait_send()

    def chunk(xs):
        return pl.ds(pl.multiple_of(xs * rows_chunk, rows_chunk), rows_chunk)

    def compute_hidden(batch, xs):
        rows = chunk(xs)

        @pl.loop(0, half_units // cols_tile)
        def _(tile):
            at = pl.ds(pl.multiple_of(tile * cols_tile, cols_tile), cols_tile)
            block = g[batch, rows, pl.ds(0, width)]
            gate_act = jnp.dot(block, gate_w[:, at], preferred_element_type=jnp.float32)
            up_act = jnp.dot(block, up_w[:, at], preferred_element_type=jnp.float32)
            hidden[:, at] = (jax.nn.silu(gate_act) * up_act).astype(jnp.bfloat16)

    def compute_down(batch, xs):
        rows = chunk(xs)
        lane = lax.broadcasted_iota(jnp.int32, (rows_chunk, 128), 1)
        weights = g[batch, rows, pl.ds(width, 128)].astype(jnp.float32)
        chosen = jnp.logical_or(lane == expert, lane == expert + 64)
        scale = jnp.sum(jnp.where(chosen, weights, 0.0), axis=1, keepdims=True)

        @pl.loop(0, width // cols_tile)
        def _(tile):
            at = pl.ds(pl.multiple_of(tile * cols_tile, cols_tile), cols_tile)
            partial = jnp.dot(hidden[...], down_w[:, at], preferred_element_type=jnp.float32)
            p[batch, rows, at] = (partial * scale).astype(jnp.bfloat16)

        for zs in range(lines_z):
            core_copy(batch, xs, zs).start()

    def core_copy(batch, xs, zs):
        index = xs * lines_z + zs
        return pltpu.make_async_remote_copy(
            src_ref=p.at[batch, at_rows(slot(xs, zs, other_core))],
            dst_ref=core_in.at[batch, at_rows(index)],
            send_sem=c_send.at[batch, index], recv_sem=c_recv.at[batch, index],
            device_id=to_core, device_id_type=MESH,
        )

    def x_copy(batch, zs, span):
        return remote(
            p.at[batch, at_rows(slot(other_x, zs, core)), span], x_in.at[batch, at_rows(zs), span],
            x_send.at[batch, zs], x_recv.at[batch, zs], to_x,
        )

    def z_copy(batch, zs, place, target):
        return remote(
            p.at[batch, at_rows(slot(x, zs, core))], z_in.at[batch, at_rows(place)],
            z_send.at[batch, zs], z_recv.at[batch, place], target,
        )

    def side_copy(batch, zs, place, target):
        return remote(
            p.at[batch, at_rows(slot(other_x, zs, core)), p_side], b_in.at[batch, at_rows(place)],
            b_send.at[batch, zs], b_recv.at[batch, place], target,
        )

    def add(batch, index, span, source, place, source_span):
        @pl.loop(0, tok // 16)
        def _(part):
            to = pl.ds(pl.multiple_of(index * tok + part * 16, 16), 16)
            of = pl.ds(pl.multiple_of(place * tok + part * 16, 16), 16)
            p[batch, to, span] = p[batch, to, span] + source[batch, of, source_span]

    def core_add(batch, xs, zs):
        core_copy(batch, xs, zs).wait_recv()
        add(batch, slot(xs, zs, core), everything, core_in, xs * lines_z + zs, everything)

    def in_order(body, steps=(0, 1, 2)):
        for zs, way in [z_steps[2 * step + side] for step in steps for side in range(2)]:
            @pl.when(z < zs if way > 0 else z > zs)
            def _():
                body(zs, way)

    def send_x(batch):
        def one(zs, way):
            core_add(batch, other_x, zs)
            x_copy(batch, zs, p_main).start()

        in_order(one)
        core_add(batch, other_x, z)

    def keep_x(batch):
        @pl.loop(0, lines_z)
        def _(zs):
            core_add(batch, x, zs)

    def line_step(batch, zs, way, copy, index, span, source, source_span):
        if way > 0:
            @pl.when(z > 0)
            def _():
                copy(batch, zs, zs, to_high).wait_recv()
                add(batch, index, span, source, zs, source_span)

            copy(batch, zs, zs, to_high).start()
        else:
            @pl.when(z < lines_z - 1)
            def _():
                copy(batch, zs, zs, to_low).wait_recv()
                add(batch, index, span, source, zs, source_span)

            place = jnp.where(z == zs + 1, lines_z, zs)
            copy(batch, zs, place, to_low).start()

    def line_end(batch, copy, index, span, source, source_span):
        @pl.when(z > 0)
        def _():
            copy(batch, z, z, to_high).wait_recv()
            add(batch, index, span, source, z, source_span)

        @pl.when(z < lines_z - 1)
        def _():
            copy(batch, z, lines_z, to_low).wait_recv()
            add(batch, index, span, source, lines_z, source_span)

    def sum_side(batch, steps):
        whole_side = pl.ds(0, side_cols)

        def one(zs, way):
            index = slot(other_x, zs, core)
            line_step(batch, zs, way, side_copy, index, p_side, b_in, whole_side)

        in_order(one, steps)

    def side_end(batch):
        line_end(batch, side_copy, slot(other_x, z, core), p_side, b_in, pl.ds(0, side_cols))
        x_copy(batch, z, everything).start()

    def sum_z(batch, steps):
        def one(zs, way):
            x_copy(batch, zs, p_main).wait_recv()
            index = slot(x, zs, core)
            add(batch, index, p_main, x_in, zs, p_main)
            line_step(batch, zs, way, z_copy, index, everything, z_in, everything)

        in_order(one, steps)

    def sum_end(batch):
        x_copy(batch, z, everything).wait_recv()
        add(batch, mine, everything, x_in, z, everything)
        line_end(batch, z_copy, mine, everything, z_in, everything)
        out[batch] = p[batch, at_rows(mine), :]

    def reduce_sent(batch):
        @pl.loop(0, lines_z)
        def _(zs):
            core_copy(batch, 0, zs).wait_send()
            core_copy(batch, 1, zs).wait_send()

            @pl.when(zs == z)
            def _():
                x_copy(batch, zs, everything).wait_send()

            @pl.when(zs != z)
            def _():
                x_copy(batch, zs, p_main).wait_send()
                z_copy(batch, zs, zs, to_x).wait_send()
                side_copy(batch, zs, zs, to_x).wait_send()

    gather_own_x(0)
    gather_own(0)
    across_own(0)
    gather_forward(0, 1)
    gather_own_x(1)
    forward_side(0, 1)
    gather_forward(0, 2)
    forward_side(0, 2)
    gather_own(1)
    gather_forward(0, 3)
    forward_side(0, 3)
    gather_core(0, x)
    for load in loads[2:]:
        load.wait()
    compute_hidden(0, x)
    gather_across(0, 1)
    across_own(1)
    compute_down(0, x)
    gather_forward(1, 1)
    gather_across(0, 2)
    forward_side(1, 1)
    gather_across(0, 3)
    gather_forward(1, 2)
    forward_side(1, 2)
    gather_core(0, other_x)
    compute_hidden(0, other_x)
    gather_forward(1, 3)
    forward_side(1, 3)
    compute_down(0, other_x)
    send_x(0)
    keep_x(0)
    sum_side(0, (0,))
    gather_core(1, x)
    gather_across(1, 1)
    compute_hidden(1, x)
    sum_side(0, (1,))
    gather_across(1, 2)
    compute_down(1, x)
    sum_side(0, (2,))
    gather_across(1, 3)
    side_end(0)
    gather_core(1, other_x)
    compute_hidden(1, other_x)
    compute_down(1, other_x)
    sum_z(0, (0,))
    send_x(1)
    sum_side(1, (0,))
    sum_z(0, (1,))
    sum_side(1, (1,))
    keep_x(1)
    sum_z(0, (2,))
    sum_side(1, (2,))
    side_end(1)
    sum_end(0)
    sum_z(1, (0, 1, 2))
    sum_end(1)
    for batch in range(batches):
        gather_sent(batch)
        reduce_sent(batch)


def gather_shards(tokens_in, expert_ids, gate_fixed, w_gate, w_up, w_down):
    batches, tok, width = tokens_in.shape
    half_units = w_gate.shape[2]
    fixed_gate = gate_fixed.astype(jnp.float32)
    weight = route_scale * fixed_gate / jnp.sum(fixed_gate, axis=2, keepdims=True)
    named = expert_ids[:, :, :, None] == jnp.arange(64, dtype=jnp.int32)
    dense = jnp.sum(jnp.where(named, weight[:, :, :, None], 0.0), axis=2)
    high = dense.astype(jnp.bfloat16)
    low = (dense - high.astype(jnp.float32)).astype(jnp.bfloat16)
    cols = jnp.concatenate([high, low], axis=2)
    total = 16 * tok
    bf16 = jnp.bfloat16
    dma = pltpu.SemaphoreType.DMA
    anywhere = pl.BlockSpec(memory_space=pl.ANY)
    vmem = pl.BlockSpec(memory_space=pltpu.VMEM)
    return pl.pallas_call(
        gather_kernel,
        out_shape=jax.ShapeDtypeStruct((batches, tok, width), bf16),
        in_specs=[anywhere, vmem, anywhere, anywhere, anywhere],
        out_specs=vmem,
        scratch_shapes=[
            pltpu.VMEM((batches, total, width + 128), bf16),
            pltpu.VMEM((batches, total, width), bf16),
            pltpu.VMEM((batches, 8 * tok, width), bf16),
            pltpu.VMEM((batches, 4 * tok, width), bf16),
            pltpu.VMEM((batches, 5 * tok, width), bf16),
            pltpu.VMEM((batches, 5 * tok, side_cols), bf16),
            pltpu.VMEM((width, half_units), bf16),
            pltpu.VMEM((width, half_units), bf16),
            pltpu.VMEM((half_units, width), bf16),
            pltpu.VMEM((rows_chunk, half_units), bf16),
            dma((5,)),
            dma((batches, 4, 16)),
            dma((batches, 16)),
            dma((batches, 16)),
            dma((batches, 8)),
            dma((batches, 8)),
            dma((batches, 4)),
            dma((batches, 4)),
            dma((batches, 4)),
            dma((batches, 5)),
            dma((batches, 4)),
            dma((batches, 5)),
        ],
        compiler_params=pltpu.CompilerParams(
            collective_id=0, has_side_effects=True, vmem_limit_bytes=63 * 1024 * 1024
        ),
        cost_estimate=pl.CostEstimate(
            flops=6 * batches * total * width * half_units,
            bytes_accessed=3 * 2 * width * half_units,
            transcendentals=batches * total * half_units,
        ),
    )(tokens_in, cols, w_gate, w_up, w_down)


def solution(mesh):
    small = mesh.shape["node"] == 4 and mesh.shape["local"] == lines_z
    return jax.shard_map(
        gather_shards if small else shards,
        mesh=mesh,
        in_specs=(
            P(None, ("groups", "node", "local"), None),
            P(None, ("groups", "node", "local"), None),
            P(None, ("groups", "node", "local"), None),
            P(("node", "local"), None, None),
            P(("node", "local"), None, None),
            P(("node", "local"), None, None),
        ),
        out_specs=P(None, ("groups", "node", "local"), None),
        check_vma=False,
    )
```

```python
import functools

import jax
import jax.numpy as jnp
from jax import lax
from jax.experimental import pallas as pl
from jax.experimental.pallas import tpu as pltpu
from jax.sharding import PartitionSpec as P

MESH = pl.DeviceIdType.MESH
lines_z = 4
rows_chunk = 512
cols_tile = 512
side_cols = 256
side_gather = 384

route_scale = 2.5


def expert_part(block, gate_half, up_half, down_half):
    block_shape = block.shape
    expert_rows = block.reshape(-1, block_shape[-1])
    gate_act = jnp.dot(expert_rows, gate_half, preferred_element_type=jnp.float32)
    up_act = jnp.dot(expert_rows, up_half, preferred_element_type=jnp.float32)
    hidden = (jax.nn.silu(gate_act) * up_act).astype(jnp.bfloat16)
    partial_out = jnp.dot(hidden, down_half, preferred_element_type=jnp.float32).astype(
        jnp.bfloat16
    )
    return partial_out.reshape(block_shape)


def shards(tokens_in, expert_ids, gate_fixed, w_gate, w_up, w_down):
    node_count = lax.axis_size("node")
    local_count = lax.axis_size("local")
    experts_node = local_count // 2
    experts = node_count * experts_node
    batches, tok_rows, width = tokens_in.shape
    top_count = expert_ids.shape[2]
    capacity = 5 * tok_rows * top_count // (4 * experts)
    gate_half = w_gate[0]
    up_half = w_up[0]
    down_half = w_down[0]
    results = []
    for micro_batch in range(batches):
        chosen = expert_ids[micro_batch]
        fixed_gate = gate_fixed[micro_batch].astype(jnp.float32)
        weight = route_scale * fixed_gate / jnp.sum(fixed_gate, axis=1, keepdims=True)
        onehot = (chosen[:, :, None] == jnp.arange(experts, dtype=jnp.int32)[None, None, :]).astype(
            jnp.int32
        )
        onehot = onehot.reshape(tok_rows * top_count, experts)
        before = jnp.cumsum(onehot, axis=0) - onehot
        slot_rank = jnp.sum(before * onehot, axis=1).reshape(tok_rows, top_count)
        position = chosen * capacity + slot_rank
        select = jnp.any(
            position[None, :, :] == jnp.arange(experts * capacity, dtype=jnp.int32)[:, None, None],
            axis=2,
        )
        packed = jnp.dot(
            select.astype(jnp.bfloat16), tokens_in[micro_batch], preferred_element_type=jnp.float32
        ).astype(jnp.bfloat16)
        blocks_grid = packed.reshape(node_count, experts_node, capacity, width)
        copies = jnp.repeat(blocks_grid, 2, axis=1).reshape(
            node_count * local_count, capacity, width
        )
        partial_value = expert_part(
            lax.all_to_all(copies, ("node", "local"), split_axis=0, concat_axis=0, tiled=True),
            gate_half,
            up_half,
            down_half,
        )
        partial_value = partial_value.reshape(node_count, local_count, capacity, width)
        returned = lax.all_to_all(
            partial_value.reshape(node_count * local_count, capacity, width),
            ("node", "local"),
            split_axis=0,
            concat_axis=0,
            tiled=True,
        )
        halves = returned.reshape(node_count, experts_node, 2, capacity, width).astype(jnp.float32)
        outputs = (halves[:, :, 0] + halves[:, :, 1]).astype(jnp.bfloat16)
        lookup = outputs.reshape(experts * capacity, width)
        picked = (
            lookup[position.reshape(-1)].reshape(tok_rows, top_count, width).astype(jnp.float32)
        )
        mixed = jnp.sum(weight[:, :, None] * picked, axis=1)
        results.append(mixed.astype(jnp.bfloat16))
    return jnp.stack(results)


z_steps = (
    ((3, 1, 0, 1), (0, -1, 2, 3)),
    ((2, 1, 0, 1), (1, -1, 2, 3)),
    ((1, 1, 0, 0), (2, -1, 3, 3), (0, -1, 1, 1), (3, 1, 2, 2)),
)


def gather_kernel(
    tokens, ids, gates, gate_hbm, up_hbm, down_hbm, out,
    g, p, core_in, x_in, z_in, b_in, gate_w, up_w, down_w, hidden,
    load_sem, g_send, g_recv, gb_recv, c_send, c_recv, x_send, x_recv, z_send, z_recv, b_send, b_recv,
):
    batches, tok, width = tokens.shape
    half_units = gate_w.shape[1]
    group = lax.axis_index("groups")
    node = lax.axis_index("node")
    z = lax.axis_index("local")
    x, core = node // 2, node % 2
    expert = node * (lines_z // 2) + z // 2
    other_x, other_core = 1 - x, 1 - core
    g_main = pl.ds(0, width + 128 - side_gather)
    g_side = pl.ds(width + 128 - side_gather, side_gather)
    p_main, p_side = pl.ds(0, width - side_cols), pl.ds(width - side_cols, side_cols)
    everything = pl.ds(0, width)
    to_x = (group, other_x * 2 + core, z)
    to_core = (group, x * 2 + other_core, z)
    to_high = (group, node, z + 1)
    to_low = (group, node, z - 1)

    def slot(xs, zs, cs):
        return (xs * lines_z + zs) * 2 + cs

    def at_rows(index):
        return pl.ds(pl.multiple_of(index * tok, tok), tok)

    mine = slot(x, z, core)
    loads = []
    for batch in range(batches):
        loads.append(
            pltpu.make_async_copy(
                tokens.at[batch], g.at[batch, at_rows(mine), pl.ds(0, width)], load_sem.at[batch]
            )
        )
    loads.append(pltpu.make_async_copy(gate_hbm.at[0], gate_w, load_sem.at[2]))
    loads.append(pltpu.make_async_copy(up_hbm.at[0], up_w, load_sem.at[3]))
    loads.append(pltpu.make_async_copy(down_hbm.at[0], down_w, load_sem.at[4]))
    for load in loads:
        load.start()
    for batch in range(batches):
        fixed_gate = gates[batch].astype(jnp.float32)
        weight = route_scale * fixed_gate / jnp.sum(fixed_gate, axis=1, keepdims=True)
        lane = lax.broadcasted_iota(jnp.int32, (tok, 128), 1)
        dense = jnp.zeros((tok, 128), jnp.float32)
        for k in range(ids.shape[2]):
            named = ids[batch, :, k : k + 1] == lane % 64
            dense += jnp.where(named, weight[:, k : k + 1], 0.0)
        high = dense.astype(jnp.bfloat16).astype(jnp.float32)
        cols = jnp.where(lane < 64, high, dense - high).astype(jnp.bfloat16)
        g[batch, at_rows(mine), pl.ds(width, 128)] = cols

    barrier = pltpu.get_barrier_semaphore()
    pl.semaphore_signal(barrier, inc=1, device_id=to_x, device_id_type=MESH)
    pl.semaphore_signal(barrier, inc=1, device_id=to_core, device_id_type=MESH)

    @pl.when(z < lines_z - 1)
    def _():
        pl.semaphore_signal(barrier, inc=1, device_id=to_high, device_id_type=MESH)

    @pl.when(z > 0)
    def _():
        pl.semaphore_signal(barrier, inc=1, device_id=to_low, device_id_type=MESH)

    pl.semaphore_wait(barrier, 3 + (z + 1) % lines_z // 2)

    def remote(part, to, send, recv, target):
        return pltpu.make_async_remote_copy(
            src_ref=part, dst_ref=to, send_sem=send, recv_sem=recv,
            device_id=target, device_id_type=MESH,
        )

    def g_copy(batch, index, kind, target):
        part = g.at[batch, at_rows(index)]
        return remote(part, part, g_send.at[batch, kind, index], g_recv.at[batch, index], target)

    def g_copy_main(batch, index):
        part = g.at[batch, at_rows(index), g_main]
        return remote(part, part, g_send.at[batch, 2, index], g_recv.at[batch, index], to_x)

    def g_copy_side(batch, index, kind, target):
        part = g.at[batch, at_rows(index), g_side]
        return remote(part, part, g_send.at[batch, kind, index], gb_recv.at[batch, index], target)

    def arrived(batch, index):
        g_copy(batch, index, 3, to_core).wait_recv()

    def both_ways(copy, batch, index):
        @pl.when(z < lines_z - 1)
        def _():
            copy(batch, index, 0, to_high).start()

        @pl.when(z > 0)
        def _():
            copy(batch, index, 1, to_low).start()

    def gather_own_x(batch):
        loads[batch].wait()
        g_copy(batch, mine, 2, to_x).start()

    def gather_own(batch):
        both_ways(g_copy, batch, mine)
        g_copy(batch, mine, 3, to_core).start()

    def gather_forward(batch, step):
        @pl.when(z >= step)
        def _():
            index = slot(x, z - step, core)
            arrived(batch, index)

            @pl.when(z < lines_z - 1)
            def _():
                g_copy(batch, index, 0, to_high).start()

            g_copy_main(batch, index).start()
            g_copy(batch, index, 3, to_core).start()

        @pl.when(z + step < lines_z)
        def _():
            index = slot(x, z + step, core)
            arrived(batch, index)

            @pl.when(z > 0)
            def _():
                g_copy(batch, index, 1, to_low).start()

            g_copy_main(batch, index).start()
            g_copy(batch, index, 3, to_core).start()

    def forward_side(batch, step):
        @pl.when(z >= step)
        def _():
            index = slot(other_x, z - step, core)
            g_copy_side(batch, index, 0, to_x).wait_recv()

            @pl.when(z < lines_z - 1)
            def _():
                g_copy_side(batch, index, 0, to_high).start()

        @pl.when(z + step < lines_z)
        def _():
            index = slot(other_x, z + step, core)
            g_copy_side(batch, index, 0, to_x).wait_recv()

            @pl.when(z > 0)
            def _():
                g_copy_side(batch, index, 1, to_low).start()

    def across_own(batch):
        index = slot(other_x, z, core)
        arrived(batch, index)
        both_ways(g_copy_side, batch, index)
        g_copy(batch, index, 3, to_core).start()

    def gather_across(batch, step):
        def one(zs):
            index = slot(other_x, zs, core)
            g_copy_main(batch, index).wait_recv()
            g_copy(batch, index, 3, to_core).start()

        @pl.when(z >= step)
        def _():
            one(z - step)

        @pl.when(z + step < lines_z)
        def _():
            one(z + step)

    def gather_core(batch, xs):
        @pl.loop(0, lines_z)
        def _(zs):
            arrived(batch, slot(xs, zs, other_core))

    def gather_sent(batch):
        @pl.loop(0, lines_z)
        def _(zs):
            index = slot(x, zs, core)
            across = slot(other_x, zs, core)

            @pl.when(jnp.logical_and(z < lines_z - 1, zs <= z))
            def _():
                g_copy(batch, index, 0, to_high).wait_send()
                g_copy_side(batch, across, 0, to_high).wait_send()

            @pl.when(jnp.logical_and(z > 0, zs >= z))
            def _():
                g_copy(batch, index, 1, to_low).wait_send()
                g_copy_side(batch, across, 1, to_low).wait_send()

            @pl.when(zs == z)
            def _():
                g_copy(batch, index, 2, to_x).wait_send()

            @pl.when(zs != z)
            def _():
                g_copy_main(batch, index).wait_send()

            g_copy(batch, index, 3, to_core).wait_send()
            g_copy(batch, across, 3, to_core).wait_send()

    def chunk(xs):
        return pl.ds(pl.multiple_of(xs * rows_chunk, rows_chunk), rows_chunk)

    def compute_hidden(batch, xs):
        rows = chunk(xs)

        @pl.loop(0, half_units // cols_tile)
        def _(tile):
            at = pl.ds(pl.multiple_of(tile * cols_tile, cols_tile), cols_tile)
            block = g[batch, rows, pl.ds(0, width)]
            gate_act = jnp.dot(block, gate_w[:, at], preferred_element_type=jnp.float32)
            up_act = jnp.dot(block, up_w[:, at], preferred_element_type=jnp.float32)
            hidden[:, at] = (jax.nn.silu(gate_act) * up_act).astype(jnp.bfloat16)

    def compute_down(batch, xs):
        rows = chunk(xs)
        lane = lax.broadcasted_iota(jnp.int32, (rows_chunk, 128), 1)
        weights = g[batch, rows, pl.ds(width, 128)].astype(jnp.float32)
        chosen = jnp.logical_or(lane == expert, lane == expert + 64)
        scale = jnp.sum(jnp.where(chosen, weights, 0.0), axis=1, keepdims=True)

        @pl.loop(0, width // cols_tile)
        def _(tile):
            at = pl.ds(pl.multiple_of(tile * cols_tile, cols_tile), cols_tile)
            partial = jnp.dot(hidden[...], down_w[:, at], preferred_element_type=jnp.float32)
            p[batch, rows, at] = (partial * scale).astype(jnp.bfloat16)

        for zs in range(lines_z):
            core_copy(batch, xs, zs).start()

    def core_copy(batch, xs, zs):
        index = xs * lines_z + zs
        return pltpu.make_async_remote_copy(
            src_ref=p.at[batch, at_rows(slot(xs, zs, other_core))],
            dst_ref=core_in.at[batch, at_rows(index)],
            send_sem=c_send.at[batch, index], recv_sem=c_recv.at[batch, index],
            device_id=to_core, device_id_type=MESH,
        )

    def x_copy(batch, zs, span):
        return remote(
            p.at[batch, at_rows(slot(other_x, zs, core)), span], x_in.at[batch, at_rows(zs), span],
            x_send.at[batch, zs], x_recv.at[batch, zs], to_x,
        )

    def z_copy(batch, zs, place, target):
        return remote(
            p.at[batch, at_rows(slot(x, zs, core))], z_in.at[batch, at_rows(place)],
            z_send.at[batch, zs], z_recv.at[batch, place], target,
        )

    def side_copy(batch, zs, place, target):
        return remote(
            p.at[batch, at_rows(slot(other_x, zs, core)), p_side], b_in.at[batch, at_rows(place)],
            b_send.at[batch, zs], b_recv.at[batch, place], target,
        )

    def add(batch, index, span, source, place, source_span):
        @pl.loop(0, tok // 16)
        def _(part):
            to = pl.ds(pl.multiple_of(index * tok + part * 16, 16), 16)
            of = pl.ds(pl.multiple_of(place * tok + part * 16, 16), 16)
            p[batch, to, span] = p[batch, to, span] + source[batch, of, source_span]

    def core_add(batch, xs, zs):
        core_copy(batch, xs, zs).wait_recv()
        add(batch, slot(xs, zs, core), everything, core_in, xs * lines_z + zs, everything)

    def in_order(body, steps=(0, 1, 2)):
        for zs, way, first, last in [entry for step in steps for entry in z_steps[step]]:
            @pl.when(jnp.logical_and(z >= first, z <= last))
            def _():
                body(zs, way)

    def send_x(batch):
        def one(zs, way):
            core_add(batch, other_x, zs)
            x_copy(batch, zs, p_main).start()

        in_order(one)
        core_add(batch, other_x, z)

    def keep_x(batch):
        @pl.loop(0, lines_z)
        def _(zs):
            core_add(batch, x, zs)

    def line_step(batch, zs, way, copy, index, span, source, source_span):
        if way > 0:
            @pl.when(z > 0)
            def _():
                copy(batch, zs, zs, to_high).wait_recv()
                add(batch, index, span, source, zs, source_span)

            copy(batch, zs, zs, to_high).start()
        else:
            @pl.when(z < lines_z - 1)
            def _():
                copy(batch, zs, zs, to_low).wait_recv()
                add(batch, index, span, source, zs, source_span)

            place = jnp.where(z == zs + 1, lines_z, zs)
            copy(batch, zs, place, to_low).start()

    def line_end(batch, copy, index, span, source, source_span):
        @pl.when(z > 0)
        def _():
            copy(batch, z, z, to_high).wait_recv()
            add(batch, index, span, source, z, source_span)

        @pl.when(z < lines_z - 1)
        def _():
            copy(batch, z, lines_z, to_low).wait_recv()
            add(batch, index, span, source, lines_z, source_span)

    def sum_side(batch, steps):
        whole_side = pl.ds(0, side_cols)

        def one(zs, way):
            index = slot(other_x, zs, core)
            line_step(batch, zs, way, side_copy, index, p_side, b_in, whole_side)

        in_order(one, steps)

    def side_end(batch):
        line_end(batch, side_copy, slot(other_x, z, core), p_side, b_in, pl.ds(0, side_cols))
        x_copy(batch, z, everything).start()

    def sum_z(batch, steps):
        def one(zs, way):
            x_copy(batch, zs, p_main).wait_recv()
            index = slot(x, zs, core)
            add(batch, index, p_main, x_in, zs, p_main)
            line_step(batch, zs, way, z_copy, index, everything, z_in, everything)

        in_order(one, steps)

    def sum_end(batch):
        x_copy(batch, z, everything).wait_recv()
        add(batch, mine, everything, x_in, z, everything)
        line_end(batch, z_copy, mine, everything, z_in, everything)
        out[batch] = p[batch, at_rows(mine), :]

    def reduce_sent(batch):
        @pl.loop(0, lines_z)
        def _(zs):
            core_copy(batch, 0, zs).wait_send()
            core_copy(batch, 1, zs).wait_send()

            @pl.when(zs == z)
            def _():
                x_copy(batch, zs, everything).wait_send()

            @pl.when(zs != z)
            def _():
                x_copy(batch, zs, p_main).wait_send()
                z_copy(batch, zs, zs, to_x).wait_send()
                side_copy(batch, zs, zs, to_x).wait_send()

    gather_own_x(0)
    gather_own(0)
    across_own(0)
    gather_forward(0, 1)
    gather_own_x(1)
    forward_side(0, 1)
    gather_forward(0, 2)
    forward_side(0, 2)
    gather_own(1)
    gather_forward(0, 3)
    forward_side(0, 3)
    gather_core(0, x)
    for load in loads[2:]:
        load.wait()
    compute_hidden(0, x)
    gather_across(0, 1)
    across_own(1)
    compute_down(0, x)
    gather_forward(1, 1)
    gather_across(0, 2)
    forward_side(1, 1)
    gather_across(0, 3)
    gather_forward(1, 2)
    forward_side(1, 2)
    gather_core(0, other_x)
    compute_hidden(0, other_x)
    gather_forward(1, 3)
    forward_side(1, 3)
    compute_down(0, other_x)
    send_x(0)
    keep_x(0)
    sum_side(0, (0,))
    gather_core(1, x)
    gather_across(1, 1)
    compute_hidden(1, x)
    sum_side(0, (1,))
    gather_across(1, 2)
    compute_down(1, x)
    sum_side(0, (2,))
    gather_across(1, 3)
    side_end(0)
    gather_core(1, other_x)
    compute_hidden(1, other_x)
    compute_down(1, other_x)
    send_x(1)
    sum_z(0, (0,))
    sum_side(1, (0,))
    sum_z(0, (1,))
    sum_side(1, (1,))
    keep_x(1)
    sum_z(0, (2,))
    sum_side(1, (2,))
    side_end(1)
    sum_end(0)
    sum_z(1, (0, 1, 2))
    sum_end(1)
    for batch in range(batches):
        gather_sent(batch)
        reduce_sent(batch)


def gather_shards(tokens_in, expert_ids, gate_fixed, w_gate, w_up, w_down):
    batches, tok, width = tokens_in.shape
    half_units = w_gate.shape[2]
    total = 16 * tok
    bf16 = jnp.bfloat16
    dma = pltpu.SemaphoreType.DMA
    anywhere = pl.BlockSpec(memory_space=pl.ANY)
    vmem = pl.BlockSpec(memory_space=pltpu.VMEM)
    return pl.pallas_call(
        gather_kernel,
        out_shape=jax.ShapeDtypeStruct((batches, tok, width), bf16),
        in_specs=[anywhere, vmem, vmem, anywhere, anywhere, anywhere],
        out_specs=vmem,
        scratch_shapes=[
            pltpu.VMEM((batches, total, width + 128), bf16),
            pltpu.VMEM((batches, total, width), bf16),
            pltpu.VMEM((batches, 8 * tok, width), bf16),
            pltpu.VMEM((batches, 4 * tok, width), bf16),
            pltpu.VMEM((batches, 5 * tok, width), bf16),
            pltpu.VMEM((batches, 5 * tok, side_cols), bf16),
            pltpu.VMEM((width, half_units), bf16),
            pltpu.VMEM((width, half_units), bf16),
            pltpu.VMEM((half_units, width), bf16),
            pltpu.VMEM((rows_chunk, half_units), bf16),
            dma((5,)),
            dma((batches, 4, 16)),
            dma((batches, 16)),
            dma((batches, 16)),
            dma((batches, 8)),
            dma((batches, 8)),
            dma((batches, 4)),
            dma((batches, 4)),
            dma((batches, 4)),
            dma((batches, 5)),
            dma((batches, 4)),
            dma((batches, 5)),
        ],
        compiler_params=pltpu.CompilerParams(
            collective_id=0, has_side_effects=True, vmem_limit_bytes=63 * 1024 * 1024
        ),
        cost_estimate=pl.CostEstimate(
            flops=6 * batches * total * width * half_units,
            bytes_accessed=3 * 2 * width * half_units,
            transcendentals=batches * total * half_units,
        ),
    )(tokens_in, expert_ids, gate_fixed, w_gate, w_up, w_down)


def solution(mesh):
    small = mesh.shape["node"] == 4 and mesh.shape["local"] == lines_z
    return jax.shard_map(
        gather_shards if small else shards,
        mesh=mesh,
        in_specs=(
            P(None, ("groups", "node", "local"), None),
            P(None, ("groups", "node", "local"), None),
            P(None, ("groups", "node", "local"), None),
            P(("node", "local"), None, None),
            P(("node", "local"), None, None),
            P(("node", "local"), None, None),
        ),
        out_specs=P(None, ("groups", "node", "local"), None),
        check_vma=False,
    )
```

```python
import functools

import jax
import jax.numpy as jnp
from jax import lax
from jax.experimental import pallas as pl
from jax.experimental.pallas import tpu as pltpu
from jax.sharding import PartitionSpec as P

MESH = pl.DeviceIdType.MESH
lines_z = 4
rows_chunk = 512
cols_tile = 512
side_cols = 256
side_gather = 384

route_scale = 2.5


def expert_part(block, gate_half, up_half, down_half):
    block_shape = block.shape
    expert_rows = block.reshape(-1, block_shape[-1])
    gate_act = jnp.dot(expert_rows, gate_half, preferred_element_type=jnp.float32)
    up_act = jnp.dot(expert_rows, up_half, preferred_element_type=jnp.float32)
    hidden = (jax.nn.silu(gate_act) * up_act).astype(jnp.bfloat16)
    partial_out = jnp.dot(hidden, down_half, preferred_element_type=jnp.float32).astype(
        jnp.bfloat16
    )
    return partial_out.reshape(block_shape)


def shards(tokens_in, expert_ids, gate_fixed, w_gate, w_up, w_down):
    node_count = lax.axis_size("node")
    local_count = lax.axis_size("local")
    experts_node = local_count // 2
    experts = node_count * experts_node
    batches, tok_rows, width = tokens_in.shape
    top_count = expert_ids.shape[2]
    capacity = 5 * tok_rows * top_count // (4 * experts)
    gate_half = w_gate[0]
    up_half = w_up[0]
    down_half = w_down[0]
    results = []
    for micro_batch in range(batches):
        chosen = expert_ids[micro_batch]
        fixed_gate = gate_fixed[micro_batch].astype(jnp.float32)
        weight = route_scale * fixed_gate / jnp.sum(fixed_gate, axis=1, keepdims=True)
        onehot = (chosen[:, :, None] == jnp.arange(experts, dtype=jnp.int32)[None, None, :]).astype(
            jnp.int32
        )
        onehot = onehot.reshape(tok_rows * top_count, experts)
        before = jnp.cumsum(onehot, axis=0) - onehot
        slot_rank = jnp.sum(before * onehot, axis=1).reshape(tok_rows, top_count)
        position = chosen * capacity + slot_rank
        select = jnp.any(
            position[None, :, :] == jnp.arange(experts * capacity, dtype=jnp.int32)[:, None, None],
            axis=2,
        )
        packed = jnp.dot(
            select.astype(jnp.bfloat16), tokens_in[micro_batch], preferred_element_type=jnp.float32
        ).astype(jnp.bfloat16)
        blocks_grid = packed.reshape(node_count, experts_node, capacity, width)
        copies = jnp.repeat(blocks_grid, 2, axis=1).reshape(
            node_count * local_count, capacity, width
        )
        partial_value = expert_part(
            lax.all_to_all(copies, ("node", "local"), split_axis=0, concat_axis=0, tiled=True),
            gate_half,
            up_half,
            down_half,
        )
        partial_value = partial_value.reshape(node_count, local_count, capacity, width)
        returned = lax.all_to_all(
            partial_value.reshape(node_count * local_count, capacity, width),
            ("node", "local"),
            split_axis=0,
            concat_axis=0,
            tiled=True,
        )
        halves = returned.reshape(node_count, experts_node, 2, capacity, width).astype(jnp.float32)
        outputs = (halves[:, :, 0] + halves[:, :, 1]).astype(jnp.bfloat16)
        lookup = outputs.reshape(experts * capacity, width)
        picked = (
            lookup[position.reshape(-1)].reshape(tok_rows, top_count, width).astype(jnp.float32)
        )
        mixed = jnp.sum(weight[:, :, None] * picked, axis=1)
        results.append(mixed.astype(jnp.bfloat16))
    return jnp.stack(results)


z_steps = (
    ((3, 1, 0, 1), (0, -1, 2, 3)),
    ((2, 1, 0, 1), (1, -1, 2, 3)),
    ((1, 1, 0, 0), (2, -1, 3, 3), (0, -1, 1, 1), (3, 1, 2, 2)),
)


def gather_kernel(
    tokens, ids, gates, gate_hbm, up_hbm, down_hbm, out,
    g, p, core_in, x_in, z_in, b_in, gate_w, up_w, down_w, hidden,
    load_sem, g_send, g_recv, gb_recv, c_send, c_recv, x_send, x_recv, z_send, z_recv, b_send, b_recv,
):
    batches, tok, width = tokens.shape
    half_units = gate_w.shape[1]
    group = lax.axis_index("groups")
    node = lax.axis_index("node")
    z = lax.axis_index("local")
    x, core = node // 2, node % 2
    expert = node * (lines_z // 2) + z // 2
    other_x, other_core = 1 - x, 1 - core
    g_main = pl.ds(0, width + 128 - side_gather)
    g_side = pl.ds(width + 128 - side_gather, side_gather)
    p_main, p_side = pl.ds(0, width - side_cols), pl.ds(width - side_cols, side_cols)
    everything = pl.ds(0, width)
    to_x = (group, other_x * 2 + core, z)
    to_core = (group, x * 2 + other_core, z)
    to_high = (group, node, z + 1)
    to_low = (group, node, z - 1)

    def slot(xs, zs, cs):
        return (xs * lines_z + zs) * 2 + cs

    def at_rows(index):
        return pl.ds(pl.multiple_of(index * tok, tok), tok)

    mine = slot(x, z, core)
    loads = []
    for batch in range(batches):
        loads.append(
            pltpu.make_async_copy(
                tokens.at[batch], g.at[batch, at_rows(mine), pl.ds(0, width)], load_sem.at[batch]
            )
        )
    loads.append(pltpu.make_async_copy(gate_hbm.at[0], gate_w, load_sem.at[2]))
    loads.append(pltpu.make_async_copy(up_hbm.at[0], up_w, load_sem.at[3]))
    loads.append(pltpu.make_async_copy(down_hbm.at[0], down_w, load_sem.at[4]))
    for load in loads:
        load.start()
    for batch in range(batches):
        fixed_gate = gates[batch].astype(jnp.float32)
        weight = route_scale * fixed_gate / jnp.sum(fixed_gate, axis=1, keepdims=True)
        lane = lax.broadcasted_iota(jnp.int32, (tok, 128), 1)
        dense = jnp.zeros((tok, 128), jnp.float32)
        for k in range(ids.shape[2]):
            named = ids[batch, :, k : k + 1] == lane % 64
            dense += jnp.where(named, weight[:, k : k + 1], 0.0)
        high = dense.astype(jnp.bfloat16).astype(jnp.float32)
        cols = jnp.where(lane < 64, high, dense - high).astype(jnp.bfloat16)
        g[batch, at_rows(mine), pl.ds(width, 128)] = cols

    barrier = pltpu.get_barrier_semaphore()
    pl.semaphore_signal(barrier, inc=1, device_id=to_x, device_id_type=MESH)
    pl.semaphore_signal(barrier, inc=1, device_id=to_core, device_id_type=MESH)

    @pl.when(z < lines_z - 1)
    def _():
        pl.semaphore_signal(barrier, inc=1, device_id=to_high, device_id_type=MESH)

    @pl.when(z > 0)
    def _():
        pl.semaphore_signal(barrier, inc=1, device_id=to_low, device_id_type=MESH)

    pl.semaphore_wait(barrier, 3 + (z + 1) % lines_z // 2)

    def remote(part, to, send, recv, target):
        return pltpu.make_async_remote_copy(
            src_ref=part, dst_ref=to, send_sem=send, recv_sem=recv,
            device_id=target, device_id_type=MESH,
        )

    def g_copy(batch, index, kind, target):
        part = g.at[batch, at_rows(index)]
        return remote(part, part, g_send.at[batch, kind, index], g_recv.at[batch, index], target)

    def g_copy_main(batch, index):
        part = g.at[batch, at_rows(index), g_main]
        return remote(part, part, g_send.at[batch, 2, index], g_recv.at[batch, index], to_x)

    def g_copy_side(batch, index, kind, target):
        part = g.at[batch, at_rows(index), g_side]
        return remote(part, part, g_send.at[batch, kind, index], gb_recv.at[batch, index], target)

    def arrived(batch, index):
        g_copy(batch, index, 3, to_core).wait_recv()

    def both_ways(copy, batch, index):
        @pl.when(z < lines_z - 1)
        def _():
            copy(batch, index, 0, to_high).start()

        @pl.when(z > 0)
        def _():
            copy(batch, index, 1, to_low).start()

    def gather_own_x(batch):
        loads[batch].wait()
        g_copy(batch, mine, 2, to_x).start()

    def gather_own(batch):
        both_ways(g_copy, batch, mine)
        g_copy(batch, mine, 3, to_core).start()

    def gather_forward(batch, step):
        @pl.when(z >= step)
        def _():
            index = slot(x, z - step, core)
            arrived(batch, index)

            @pl.when(z < lines_z - 1)
            def _():
                g_copy(batch, index, 0, to_high).start()

            g_copy_main(batch, index).start()
            g_copy(batch, index, 3, to_core).start()

        @pl.when(z + step < lines_z)
        def _():
            index = slot(x, z + step, core)
            arrived(batch, index)

            @pl.when(z > 0)
            def _():
                g_copy(batch, index, 1, to_low).start()

            g_copy_main(batch, index).start()
            g_copy(batch, index, 3, to_core).start()

    def forward_side(batch, step):
        @pl.when(z >= step)
        def _():
            index = slot(other_x, z - step, core)
            g_copy_side(batch, index, 0, to_x).wait_recv()

            @pl.when(z < lines_z - 1)
            def _():
                g_copy_side(batch, index, 0, to_high).start()

        @pl.when(z + step < lines_z)
        def _():
            index = slot(other_x, z + step, core)
            g_copy_side(batch, index, 0, to_x).wait_recv()

            @pl.when(z > 0)
            def _():
                g_copy_side(batch, index, 1, to_low).start()

    def across_own(batch):
        index = slot(other_x, z, core)
        arrived(batch, index)
        both_ways(g_copy_side, batch, index)
        g_copy(batch, index, 3, to_core).start()

    def gather_across(batch, step):
        def one(zs):
            index = slot(other_x, zs, core)
            g_copy_main(batch, index).wait_recv()
            g_copy(batch, index, 3, to_core).start()

        @pl.when(z >= step)
        def _():
            one(z - step)

        @pl.when(z + step < lines_z)
        def _():
            one(z + step)

    def gather_core(batch, xs):
        @pl.loop(0, lines_z)
        def _(zs):
            arrived(batch, slot(xs, zs, other_core))

    def gather_sent(batch):
        @pl.loop(0, lines_z)
        def _(zs):
            index = slot(x, zs, core)
            across = slot(other_x, zs, core)

            @pl.when(jnp.logical_and(z < lines_z - 1, zs <= z))
            def _():
                g_copy(batch, index, 0, to_high).wait_send()
                g_copy_side(batch, across, 0, to_high).wait_send()

            @pl.when(jnp.logical_and(z > 0, zs >= z))
            def _():
                g_copy(batch, index, 1, to_low).wait_send()
                g_copy_side(batch, across, 1, to_low).wait_send()

            @pl.when(zs == z)
            def _():
                g_copy(batch, index, 2, to_x).wait_send()

            @pl.when(zs != z)
            def _():
                g_copy_main(batch, index).wait_send()

            g_copy(batch, index, 3, to_core).wait_send()
            g_copy(batch, across, 3, to_core).wait_send()

    def chunk(xs):
        return pl.ds(pl.multiple_of(xs * rows_chunk, rows_chunk), rows_chunk)

    def compute_hidden(batch, xs):
        rows = chunk(xs)

        @pl.loop(0, half_units // cols_tile)
        def _(tile):
            at = pl.ds(pl.multiple_of(tile * cols_tile, cols_tile), cols_tile)
            block = g[batch, rows, pl.ds(0, width)]
            gate_act = jnp.dot(block, gate_w[:, at], preferred_element_type=jnp.float32)
            up_act = jnp.dot(block, up_w[:, at], preferred_element_type=jnp.float32)
            hidden[:, at] = (jax.nn.silu(gate_act) * up_act).astype(jnp.bfloat16)

    def compute_down(batch, xs):
        rows = chunk(xs)
        lane = lax.broadcasted_iota(jnp.int32, (rows_chunk, 128), 1)
        weights = g[batch, rows, pl.ds(width, 128)].astype(jnp.float32)
        chosen = jnp.logical_or(lane == expert, lane == expert + 64)
        scale = jnp.sum(jnp.where(chosen, weights, 0.0), axis=1, keepdims=True)

        @pl.loop(0, width // cols_tile)
        def _(tile):
            at = pl.ds(pl.multiple_of(tile * cols_tile, cols_tile), cols_tile)
            partial = jnp.dot(hidden[...], down_w[:, at], preferred_element_type=jnp.float32)
            p[batch, rows, at] = (partial * scale).astype(jnp.bfloat16)

        for zs in range(lines_z):
            core_copy(batch, xs, zs).start()

    def core_copy(batch, xs, zs):
        index = xs * lines_z + zs
        return pltpu.make_async_remote_copy(
            src_ref=p.at[batch, at_rows(slot(xs, zs, other_core))],
            dst_ref=core_in.at[batch, at_rows(index)],
            send_sem=c_send.at[batch, index], recv_sem=c_recv.at[batch, index],
            device_id=to_core, device_id_type=MESH,
        )

    def x_copy(batch, zs, span):
        return remote(
            p.at[batch, at_rows(slot(other_x, zs, core)), span], x_in.at[batch, at_rows(zs), span],
            x_send.at[batch, zs], x_recv.at[batch, zs], to_x,
        )

    def z_copy(batch, zs, place, target):
        return remote(
            p.at[batch, at_rows(slot(x, zs, core))], z_in.at[batch, at_rows(place)],
            z_send.at[batch, zs], z_recv.at[batch, place], target,
        )

    def side_copy(batch, zs, place, target):
        return remote(
            p.at[batch, at_rows(slot(other_x, zs, core)), p_side], b_in.at[batch, at_rows(place)],
            b_send.at[batch, zs], b_recv.at[batch, place], target,
        )

    def add(batch, index, span, source, place, source_span):
        @pl.loop(0, tok // 16)
        def _(part):
            to = pl.ds(pl.multiple_of(index * tok + part * 16, 16), 16)
            of = pl.ds(pl.multiple_of(place * tok + part * 16, 16), 16)
            p[batch, to, span] = p[batch, to, span] + source[batch, of, source_span]

    def core_add(batch, xs, zs):
        core_copy(batch, xs, zs).wait_recv()
        add(batch, slot(xs, zs, core), everything, core_in, xs * lines_z + zs, everything)

    def in_order(body, steps=(0, 1, 2)):
        for zs, way, first, last in [entry for step in steps for entry in z_steps[step]]:
            @pl.when(jnp.logical_and(z >= first, z <= last))
            def _():
                body(zs, way)

    def send_x(batch):
        def one(zs, way):
            core_add(batch, other_x, zs)
            x_copy(batch, zs, p_main).start()

        in_order(one)
        core_add(batch, other_x, z)

    def keep_x(batch):
        @pl.loop(0, lines_z)
        def _(zs):
            core_add(batch, x, zs)

    def line_step(batch, zs, way, copy, index, span, source, source_span):
        if way > 0:
            @pl.when(z > 0)
            def _():
                copy(batch, zs, zs, to_high).wait_recv()
                add(batch, index, span, source, zs, source_span)

            copy(batch, zs, zs, to_high).start()
        else:
            @pl.when(z < lines_z - 1)
            def _():
                copy(batch, zs, zs, to_low).wait_recv()
                add(batch, index, span, source, zs, source_span)

            place = jnp.where(z == zs + 1, lines_z, zs)
            copy(batch, zs, place, to_low).start()

    def line_end(batch, copy, index, span, source, source_span):
        @pl.when(z > 0)
        def _():
            copy(batch, z, z, to_high).wait_recv()
            add(batch, index, span, source, z, source_span)

        @pl.when(z < lines_z - 1)
        def _():
            copy(batch, z, lines_z, to_low).wait_recv()
            add(batch, index, span, source, lines_z, source_span)

    def sum_side(batch, steps):
        whole_side = pl.ds(0, side_cols)

        def one(zs, way):
            index = slot(other_x, zs, core)
            line_step(batch, zs, way, side_copy, index, p_side, b_in, whole_side)

        in_order(one, steps)

    def side_end(batch):
        line_end(batch, side_copy, slot(other_x, z, core), p_side, b_in, pl.ds(0, side_cols))
        x_copy(batch, z, everything).start()

    def sum_z(batch, steps):
        def one(zs, way):
            x_copy(batch, zs, p_main).wait_recv()
            index = slot(x, zs, core)
            add(batch, index, p_main, x_in, zs, p_main)
            line_step(batch, zs, way, z_copy, index, everything, z_in, everything)

        in_order(one, steps)

    def sum_end(batch):
        x_copy(batch, z, everything).wait_recv()
        add(batch, mine, everything, x_in, z, everything)
        line_end(batch, z_copy, mine, everything, z_in, everything)
        out[batch] = p[batch, at_rows(mine), :]

    def reduce_sent(batch):
        @pl.loop(0, lines_z)
        def _(zs):
            core_copy(batch, 0, zs).wait_send()
            core_copy(batch, 1, zs).wait_send()

            @pl.when(zs == z)
            def _():
                x_copy(batch, zs, everything).wait_send()

            @pl.when(zs != z)
            def _():
                x_copy(batch, zs, p_main).wait_send()
                z_copy(batch, zs, zs, to_x).wait_send()
                side_copy(batch, zs, zs, to_x).wait_send()

    gather_own_x(0)
    gather_own(0)
    across_own(0)
    gather_forward(0, 1)
    gather_own_x(1)
    forward_side(0, 1)
    gather_forward(0, 2)
    forward_side(0, 2)
    gather_own(1)
    gather_forward(0, 3)
    forward_side(0, 3)
    gather_core(0, x)
    for load in loads[2:]:
        load.wait()
    compute_hidden(0, x)
    gather_across(0, 1)
    across_own(1)
    compute_down(0, x)
    gather_forward(1, 1)
    gather_across(0, 2)
    forward_side(1, 1)
    gather_across(0, 3)
    gather_forward(1, 2)
    forward_side(1, 2)
    gather_core(0, other_x)
    compute_hidden(0, other_x)
    gather_forward(1, 3)
    forward_side(1, 3)
    compute_down(0, other_x)
    send_x(0)
    keep_x(0)
    sum_side(0, (0,))
    gather_core(1, x)
    gather_across(1, 1)
    compute_hidden(1, x)
    sum_side(0, (1,))
    gather_across(1, 2)
    compute_down(1, x)
    sum_side(0, (2,))
    gather_across(1, 3)
    side_end(0)
    gather_core(1, other_x)
    compute_hidden(1, other_x)
    compute_down(1, other_x)
    send_x(1)
    sum_z(0, (0,))
    sum_side(1, (0,))
    sum_z(0, (1,))
    sum_side(1, (1,))
    keep_x(1)
    sum_z(0, (2,))
    sum_side(1, (2,))
    side_end(1)
    sum_z(1, (0,))
    sum_end(0)
    sum_z(1, (1, 2))
    sum_end(1)
    for batch in range(batches):
        gather_sent(batch)
        reduce_sent(batch)


def gather_shards(tokens_in, expert_ids, gate_fixed, w_gate, w_up, w_down):
    batches, tok, width = tokens_in.shape
    half_units = w_gate.shape[2]
    total = 16 * tok
    bf16 = jnp.bfloat16
    dma = pltpu.SemaphoreType.DMA
    anywhere = pl.BlockSpec(memory_space=pl.ANY)
    vmem = pl.BlockSpec(memory_space=pltpu.VMEM)
    return pl.pallas_call(
        gather_kernel,
        out_shape=jax.ShapeDtypeStruct((batches, tok, width), bf16),
        in_specs=[anywhere, vmem, vmem, anywhere, anywhere, anywhere],
        out_specs=vmem,
        scratch_shapes=[
            pltpu.VMEM((batches, total, width + 128), bf16),
            pltpu.VMEM((batches, total, width), bf16),
            pltpu.VMEM((batches, 8 * tok, width), bf16),
            pltpu.VMEM((batches, 4 * tok, width), bf16),
            pltpu.VMEM((batches, 5 * tok, width), bf16),
            pltpu.VMEM((batches, 5 * tok, side_cols), bf16),
            pltpu.VMEM((width, half_units), bf16),
            pltpu.VMEM((width, half_units), bf16),
            pltpu.VMEM((half_units, width), bf16),
            pltpu.VMEM((rows_chunk, half_units), bf16),
            dma((5,)),
            dma((batches, 4, 16)),
            dma((batches, 16)),
            dma((batches, 16)),
            dma((batches, 8)),
            dma((batches, 8)),
            dma((batches, 4)),
            dma((batches, 4)),
            dma((batches, 4)),
            dma((batches, 5)),
            dma((batches, 4)),
            dma((batches, 5)),
        ],
        compiler_params=pltpu.CompilerParams(
            collective_id=0, has_side_effects=True, vmem_limit_bytes=63 * 1024 * 1024
        ),
        cost_estimate=pl.CostEstimate(
            flops=6 * batches * total * width * half_units,
            bytes_accessed=3 * 2 * width * half_units,
            transcendentals=batches * total * half_units,
        ),
    )(tokens_in, expert_ids, gate_fixed, w_gate, w_up, w_down)


def solution(mesh):
    small = mesh.shape["node"] == 4 and mesh.shape["local"] == lines_z
    return jax.shard_map(
        gather_shards if small else shards,
        mesh=mesh,
        in_specs=(
            P(None, ("groups", "node", "local"), None),
            P(None, ("groups", "node", "local"), None),
            P(None, ("groups", "node", "local"), None),
            P(("node", "local"), None, None),
            P(("node", "local"), None, None),
            P(("node", "local"), None, None),
        ),
        out_specs=P(None, ("groups", "node", "local"), None),
        check_vma=False,
    )
```
